32 devices in a mesh: tile: 8 (over z, y), member: 4 (over x, core).
Axes of the slice: x: 2, y: 2, z: 4, core: 2. Of those that a mesh axis runs over, the one named last changes fastest.
Arguments:
- latent: float32 [4, 4, 64, 8192], P('member', None, None, 'tile'), may hold values from -6 to 6
- noise: float32 [4, 4, 64, 8192], P('member', None, None, 'tile'), may hold values from -6 to 6
- features: bfloat16 [64, 64, 8192], P('member', None, 'tile'), may hold values from -6 to 6
- slot_window: int32 [48], P('tile'), may hold values from -1 to 254, as said below
- timestep: int32 [1], replicated, may hold values from 200 to 999
- time_weight: bfloat16 [64, 64], replicated, may hold values from -0.75 to 0.75
- in_weight: bfloat16 [64, 36], replicated, may hold values from -1 to 1
- conv1_weight: bfloat16 [64, 576], replicated, may hold values from -0.25 to 0.25
- conv2_weight: bfloat16 [64, 576], replicated, may hold values from -0.25 to 0.25
- out_weight: bfloat16 [4, 576], replicated, may hold values from -0.25 to 0.25
- norm1_gain: float32 [64], replicated, may hold values from 0.1 to 1.9
- norm2_gain: float32 [64], replicated, may hold values from 0.1 to 1.9
- norm3_gain: float32 [64], replicated, may hold values from 0.1 to 1.9
Outputs:
- latent_prev: float32 [4, 4, 64, 8192], P('member', None, None, 'tile')
The draws below stay inside these ranges and needn't reach their ends.
Inputs may be any that keep to these rules, and one draw needn't show every extreme that they name: `slot_window`: entry j of tile t's 6 slots (index t * 6 + j) is -1 for an empty slot or a window whose columns all lie in tiles t - 1 to t + 1; a window may be listed in several slots, and each listing counts.
All inputs are finite; a program needn't handle non-finite values.
Results may differ from the reference program's by a relative error of at most 0.0003.
Values may be sent and summed in bfloat16 or wider, within the bound.
A program may use at most 128 MiB of HBM per device.

```python
import math
import jax
import jax.numpy as jnp
from jax import lax

C = 64
LAT = 4
WIN = 64
SLOTS = 6
REACH = 1
TRAIN_STEPS = 1000
STRIDE = 20
GROUPS = 32
MEMBERS = 4
NX = 8192
WPT = 32
NWIN = 255
SLOTS_ALL = 48


def draw_slot_window(key, part):
    key_offset, key_within, key_keep = jax.random.split(key, 3)
    position = jnp.arange(SLOTS_ALL, dtype=jnp.int32)
    owner = position // SLOTS
    slot_rank = position % SLOTS
    offset = jax.random.randint(key_offset, (SLOTS_ALL,), -REACH, REACH + 1, dtype=jnp.int32)
    upper = jnp.where(offset == REACH, WPT - 1, WPT).astype(jnp.int32)
    within = jax.random.randint(key_within, (SLOTS_ALL,), 0, upper, dtype=jnp.int32)
    offset = jnp.where(slot_rank == 0, REACH, jnp.where(slot_rank == 1, -REACH, jnp.where(slot_rank == 2, 0, offset)))
    within = jnp.where(slot_rank == 0, WPT - 2, jnp.where(slot_rank == 1, 0, jnp.where(slot_rank == 2, WPT - 1, within)))
    chosen = (owner + offset) * WPT + within
    keeper = (jax.random.randint(key_keep, (SLOTS_ALL,), 0, 4, dtype=jnp.int32) > 0) | (slot_rank < 3)
    valid = keeper & (chosen >= 0) & (chosen < NWIN)
    return jnp.where(valid, chosen, -1).astype(jnp.int32)


def shard_levels(key, dims, cuts, low, top_value):
    def one(axis_at, parts):
        steps = jax.random.uniform(jax.random.fold_in(jax.random.fold_in(key, 6), axis_at), (parts,), jnp.float32, low / len(cuts), top_value / len(cuts))
        return jnp.repeat(jnp.exp(steps), dims[axis_at] // parts).reshape((-1,) + (1,) * (len(dims) - axis_at - 1))

    factor_of = one(*cuts[0])
    for cut in cuts[1:]:
        factor_of = factor_of * one(*cut)
    return factor_of


def normal_values(key, extent, deviation, most, pieces=(), kind=jnp.bfloat16):
    values = jax.random.normal(key, extent, jnp.float32) * deviation
    if len(pieces) > 0:
        values = shard_levels(key, extent, pieces, -0.22, 0.18) * values
    return jnp.clip(values, min=-most, max=most).astype(kind)


def setup_inputs(seed: int = 0) -> dict:
    key_of = jax.random.split(jax.random.key(seed), 14)
    return {
        "latent": normal_values(key_of[0], (MEMBERS, LAT, WIN, NX), 1.0, 6.0, ((0, 4), (3, 8)), jnp.float32),
        "noise": normal_values(key_of[1], (MEMBERS, LAT, WIN, NX), 1.0, 6.0, ((0, 4), (3, 8)), jnp.float32),
        "features": normal_values(key_of[2], (C, WIN, NX), 1.0, 6.0, ((0, 4), (2, 8))),
        "slot_window": draw_slot_window(jax.random.fold_in(key_of[13], 71), 0),
        "timestep": jax.random.randint(key_of[4], (1,), 200, 1000).astype(jnp.int32),
        "time_weight": normal_values(key_of[5], (C, C), C ** -0.5, 0.75),
        "in_weight": normal_values(key_of[6], (C, 9 * LAT), (9 * LAT) ** -0.5, 1.0),
        "conv1_weight": normal_values(key_of[7], (C, 9 * C), (9 * C) ** -0.5, 0.25),
        "conv2_weight": normal_values(key_of[8], (C, 9 * C), (9 * C) ** -0.5, 0.25),
        "out_weight": normal_values(key_of[9], (LAT, 9 * C), (9 * C) ** -0.5, 0.25),
        "norm1_gain": jnp.clip(1.0 + 0.18 * jax.random.normal(key_of[10], (C,), jnp.float32), 0.1, 1.9),
        "norm2_gain": jnp.clip(1.0 + 0.18 * jax.random.normal(key_of[11], (C,), jnp.float32), 0.1, 1.9),
        "norm3_gain": jnp.clip(1.0 + 0.18 * jax.random.normal(key_of[12], (C,), jnp.float32), 0.1, 1.9),
    }


norm_epsilon = 1e-05
eta_noise = 0.5
beta_first = 0.00085
beta_last = 0.012

def plan_terms(timestep):
    betas_root = jnp.linspace(beta_first ** 0.5, beta_last ** 0.5, TRAIN_STEPS, dtype=jnp.float32)
    alpha_bar = jnp.cumprod(1.0 - betas_root * betas_root)
    current = alpha_bar[timestep[0]]
    earlier = alpha_bar[timestep[0] - STRIDE]
    sigma_sq = eta_noise * eta_noise * (1.0 - earlier) / (1.0 - current) * (1.0 - current / earlier)
    return (current, earlier, sigma_sq)

def time_embed(timestep, time_weight):
    half_width = time_weight.shape[0] // 2
    freqs_row = jnp.exp(-math.log(10000.0) * jnp.arange(half_width, dtype=jnp.float32) / half_width)
    angles = timestep[0].astype(jnp.float32) * freqs_row
    embedding = jnp.concatenate([jnp.cos(angles), jnp.sin(angles)]).astype(jnp.bfloat16)
    return jax.nn.silu(jnp.dot(embedding[None, :], time_weight, preferred_element_type=jnp.float32)[0])

def conv_same(activation, weight, window_side):
    cell_count = activation.shape[-1]
    column = jnp.arange(cell_count, dtype=jnp.int32) % window_side
    padded = jnp.pad(activation, ((0, 0), (window_side + 1, window_side + 1)))
    tap_list = []
    for row_shift in (-1, 0, 1):
        for col_shift in (-1, 0, 1):
            anchor = window_side + 1 + row_shift * window_side + col_shift
            tap_piece = padded[:, anchor:anchor + cell_count]
            if col_shift == -1:
                tap_piece = jnp.where(column >= 1, tap_piece, jnp.zeros_like(tap_piece))
            if col_shift == 1:
                tap_piece = jnp.where(column <= window_side - 2, tap_piece, jnp.zeros_like(tap_piece))
            tap_list.append(tap_piece)
    stacked = jnp.concatenate(tap_list, axis=0)
    return jnp.dot(weight, stacked, preferred_element_type=jnp.float32)

def group_norm(hidden, gain):
    channels, cell_count = hidden.shape
    grouped = hidden.reshape(GROUPS, channels // GROUPS * cell_count)
    center = lax.optimization_barrier(jnp.mean(grouped, axis=1, keepdims=True))
    deviate = grouped - center
    spread_sq = lax.optimization_barrier(jnp.mean(deviate * deviate, axis=1, keepdims=True))
    normed = (deviate * lax.rsqrt(spread_sq + norm_epsilon)).reshape(channels, cell_count)
    return normed * gain[:, None]

def denoiser(latent_win, feature_win, time_bias, weight_set):
    in_weight, conv1_weight, conv2_weight, out_weight, gain_one, gain_two, gain_three = weight_set
    hidden = conv_same(latent_win, in_weight, WIN) + feature_win.astype(jnp.float32)
    first_act = jax.nn.silu(group_norm(hidden, gain_one)).astype(jnp.bfloat16)
    middle = conv_same(first_act, conv1_weight, WIN) + time_bias[:, None]
    second_act = jax.nn.silu(group_norm(middle, gain_two)).astype(jnp.bfloat16)
    block_out = hidden + conv_same(second_act, conv2_weight, WIN)
    third_act = jax.nn.silu(group_norm(block_out, gain_three)).astype(jnp.bfloat16)
    return conv_same(third_act, out_weight, WIN)

def denoise_update(state_now, eps_mean, noise_draw, current, earlier, sigma_sq):
    clean_est = (state_now - jnp.sqrt(1.0 - current) * eps_mean) / jnp.sqrt(current)
    return jnp.sqrt(earlier) * clean_est + jnp.sqrt(1.0 - earlier - sigma_sq) * eps_mean + jnp.sqrt(sigma_sq) * noise_draw

def reference(latent, noise, features, slot_window, timestep, time_weight, in_weight, conv1_weight, conv2_weight, out_weight, norm1_gain, norm2_gain, norm3_gain):
    half_win = WIN // 2
    window_ids = jnp.arange(NWIN, dtype=jnp.int32)
    listings = lax.optimization_barrier(jnp.sum((slot_window[:, None] == window_ids[None, :]).astype(jnp.float32), axis=0))
    columns = jnp.arange(NX, dtype=jnp.int32)
    starts = window_ids * half_win
    inside = (columns[None, :] >= starts[:, None]) & (columns[None, :] < starts[:, None] + WIN)
    cover = lax.optimization_barrier(jnp.sum(listings[:, None] * inside.astype(jnp.float32), axis=0))
    current, earlier, sigma_sq = plan_terms(timestep)
    time_bias = time_embed(timestep, time_weight)
    weight_set = (in_weight, conv1_weight, conv2_weight, out_weight, norm1_gain, norm2_gain, norm3_gain)
    results = []
    for member_index in range(MEMBERS):
        band_latent = latent[member_index].astype(jnp.bfloat16)

        def one_window(window_id):
            start_col = (window_id * half_win).astype(jnp.int32)
            latent_win = lax.dynamic_slice_in_dim(band_latent, start_col, WIN, 2).reshape(LAT, WIN * WIN)
            feature_win = lax.dynamic_slice_in_dim(features, start_col, WIN, 2).reshape(C, WIN * WIN)
            return denoiser(latent_win, feature_win, time_bias, weight_set)
        eps_windows = lax.map(one_window, window_ids)

        def add_window(running, packed):
            window_id, eps_window, listed = packed
            start_col = (window_id * half_win).astype(jnp.int32)
            current_slab = lax.dynamic_slice_in_dim(running, start_col, WIN, 2)
            updated = current_slab + listed * eps_window.reshape(LAT, WIN, WIN)
            return (lax.dynamic_update_slice_in_dim(running, updated, start_col, 2), None)
        eps_total, ignored = lax.scan(add_window, jnp.zeros((LAT, WIN, NX), jnp.float32), (window_ids, eps_windows, listings))
        eps_mean = eps_total / jnp.maximum(cover, 1.0)[None, None, :]
        results.append(denoise_update(latent[member_index], eps_mean, noise[member_index], current, earlier, sigma_sq))
    return jnp.stack(results)
```

```python
import math

import jax
import jax.numpy as jnp
from jax import lax
from jax.sharding import PartitionSpec as P

LAT = 4
WIN = 64
REACH = 1
TRAIN_STEPS = 1000
STRIDE = 20
GROUPS = 32


norm_epsilon = 1e-05
eta_noise = 0.5
beta_first = 0.00085
beta_last = 0.012


def with_halo(block, sides, width):
    for axis, dim in sides:
        count = lax.axis_size(axis)
        forward = [(i, i + 1) for i in range(count - 1)]
        backward = [(target, source) for source, target in forward]
        low = lax.ppermute(
            lax.slice_in_dim(block, block.shape[dim] - width, None, axis=dim), axis, forward
        )
        high = lax.ppermute(lax.slice_in_dim(block, 0, width, axis=dim), axis, backward)
        block = jnp.concatenate([low, block, high], axis=dim)
    return block


def from_behind(value, axis, by):
    length = lax.axis_size(axis)
    pairs = [(i, i + by) for i in range(length) if 0 <= i + by < length]
    return lax.ppermute(value, axis, pairs)


def plan_terms(timestep):
    betas_root = jnp.linspace(beta_first**0.5, beta_last**0.5, TRAIN_STEPS, dtype=jnp.float32)
    kept = 1.0 - betas_root * betas_root
    step = jnp.arange(TRAIN_STEPS, dtype=jnp.int32)
    current = jnp.prod(jnp.where(step <= timestep[0], kept, 1.0))
    earlier = jnp.prod(jnp.where(step <= timestep[0] - STRIDE, kept, 1.0))
    sigma_sq = eta_noise * eta_noise * (1.0 - earlier) / (1.0 - current) * (1.0 - current / earlier)
    return (current, earlier, sigma_sq)


def time_embed(timestep, time_weight):
    half_width = time_weight.shape[0] // 2
    freqs_row = jnp.exp(-math.log(10000.0) * jnp.arange(half_width, dtype=jnp.float32) / half_width)
    angles = timestep[0].astype(jnp.float32) * freqs_row
    embedding = jnp.concatenate([jnp.cos(angles), jnp.sin(angles)]).astype(jnp.bfloat16)
    return jax.nn.silu(
        jnp.dot(embedding[None, :], time_weight, preferred_element_type=jnp.float32)[0]
    )


def conv_same(activation, weight, window_side):
    cell_count = activation.shape[-1]
    column = jnp.arange(cell_count, dtype=jnp.int32) % window_side
    padded = jnp.pad(activation, ((0, 0), (window_side + 1, window_side + 1)))
    tap_list = []
    for row_shift in (-1, 0, 1):
        for col_shift in (-1, 0, 1):
            anchor = window_side + 1 + row_shift * window_side + col_shift
            tap_piece = padded[:, anchor : anchor + cell_count]
            if col_shift == -1:
                tap_piece = jnp.where(column >= 1, tap_piece, jnp.zeros_like(tap_piece))
            if col_shift == 1:
                tap_piece = jnp.where(
                    column <= window_side - 2, tap_piece, jnp.zeros_like(tap_piece)
                )
            tap_list.append(tap_piece)
    stacked = jnp.concatenate(tap_list, axis=0)
    return jnp.dot(weight, stacked, preferred_element_type=jnp.float32)


def group_norm(hidden, gain):
    channels, cell_count = hidden.shape
    grouped = hidden.reshape(GROUPS, channels // GROUPS * cell_count)
    center = jnp.mean(grouped, axis=1, keepdims=True)
    deviate = grouped - center
    spread_sq = jnp.mean(deviate * deviate, axis=1, keepdims=True)
    normed = (deviate * lax.rsqrt(spread_sq + norm_epsilon)).reshape(channels, cell_count)
    return normed * gain[:, None]


def denoiser(latent_win, feature_win, time_bias, weight_set):
    in_weight, conv1_weight, conv2_weight, out_weight, gain_one, gain_two, gain_three = weight_set
    hidden = conv_same(latent_win, in_weight, WIN) + feature_win.astype(jnp.float32)
    first_act = jax.nn.silu(group_norm(hidden, gain_one)).astype(jnp.bfloat16)
    middle = conv_same(first_act, conv1_weight, WIN) + time_bias[:, None]
    second_act = jax.nn.silu(group_norm(middle, gain_two)).astype(jnp.bfloat16)
    block_out = hidden + conv_same(second_act, conv2_weight, WIN)
    third_act = jax.nn.silu(group_norm(block_out, gain_three)).astype(jnp.bfloat16)
    return conv_same(third_act, out_weight, WIN)


def denoise_update(state_now, eps_mean, noise_draw, current, earlier, sigma_sq):
    clean_est = (state_now - jnp.sqrt(1.0 - current) * eps_mean) / jnp.sqrt(current)
    return (
        jnp.sqrt(earlier) * clean_est
        + jnp.sqrt(1.0 - earlier - sigma_sq) * eps_mean
        + jnp.sqrt(sigma_sq) * noise_draw
    )


def body(
    latent,
    noise,
    features,
    slot_window,
    timestep,
    time_weight,
    in_weight,
    conv1_weight,
    conv2_weight,
    out_weight,
    norm1_gain,
    norm2_gain,
    norm3_gain,
):
    tile_width = latent.shape[-1]
    half_win = WIN // 2
    rim_width = REACH * tile_width
    ext_width = tile_width + 2 * rim_width
    tile_index = lax.axis_index("tile")
    all_channels = lax.all_gather(features, "member", axis=0, tiled=True)
    driver_ext = with_halo(all_channels, (("tile", 2),), rim_width)
    latent_ext = with_halo(latent[0].astype(jnp.bfloat16), (("tile", 2),), rim_width)
    current, earlier, sigma_sq = plan_terms(timestep)
    time_bias = time_embed(timestep, time_weight)
    weight_set = (
        in_weight,
        conv1_weight,
        conv2_weight,
        out_weight,
        norm1_gain,
        norm2_gain,
        norm3_gain,
    )
    listed = slot_window >= 0
    listed_weight = listed.astype(jnp.float32)
    local_start = jnp.where(
        listed, slot_window * half_win - tile_index * tile_width + rim_width, rim_width
    )
    channels = driver_ext.shape[0]

    def one_slot(start_col):
        latent_win = lax.dynamic_slice_in_dim(latent_ext, start_col, WIN, 2).reshape(LAT, WIN * WIN)
        feature_win = lax.dynamic_slice_in_dim(driver_ext, start_col, WIN, 2).reshape(
            channels, WIN * WIN
        )
        return denoiser(latent_win, feature_win, time_bias, weight_set)

    eps_slots = lax.map(one_slot, local_start)

    def add_slot(running, packed):
        start_col, eps_window, weight_one = packed
        current_slab = lax.dynamic_slice_in_dim(running, start_col, WIN, 2)
        updated = current_slab + weight_one * eps_window.reshape(LAT, WIN, WIN)
        return (lax.dynamic_update_slice_in_dim(running, updated, start_col, 2), None)

    partial_ext, ignored = lax.scan(
        add_slot,
        jnp.zeros((LAT, WIN, ext_width), jnp.float32),
        (local_start, eps_slots, listed_weight),
    )
    ext_cols = jnp.arange(ext_width, dtype=jnp.int32)
    inside = (ext_cols[None, :] >= local_start[:, None]) & (
        ext_cols[None, :] < local_start[:, None] + WIN
    )
    cover_ext = jnp.sum(listed_weight[:, None] * inside.astype(jnp.float32), axis=0)
    eps_total = partial_ext[:, :, rim_width : rim_width + tile_width]
    cover_total = cover_ext[rim_width : rim_width + tile_width]
    distance = 1
    low_col = rim_width + distance * tile_width
    sums_piece = partial_ext[:, :, low_col : low_col + tile_width]
    count_piece = cover_ext[low_col : low_col + tile_width]
    got_sums = from_behind(sums_piece.astype(jnp.bfloat16), "tile", distance).astype(
        sums_piece.dtype
    )
    got_count = from_behind(count_piece.astype(jnp.bfloat16), "tile", distance).astype(
        count_piece.dtype
    )
    eps_total = eps_total + got_sums
    cover_total = cover_total + got_count
    distance = 1
    high_col = rim_width - (distance - 1) * tile_width
    low_col = high_col - tile_width
    sums_piece = partial_ext[:, :, low_col:high_col]
    count_piece = cover_ext[low_col:high_col]
    got_sums = from_behind(sums_piece.astype(jnp.bfloat16), "tile", -distance).astype(
        sums_piece.dtype
    )
    got_count = from_behind(count_piece.astype(jnp.bfloat16), "tile", -distance).astype(
        count_piece.dtype
    )
    eps_total = eps_total + got_sums
    cover_total = cover_total + got_count
    eps_mean = eps_total / jnp.maximum(cover_total, 1.0)[None, None, :]
    return denoise_update(latent[0], eps_mean, noise[0], current, earlier, sigma_sq)[None]


def solution(mesh):
    placed = (
        P("member", None, None, "tile"),
        P("member", None, None, "tile"),
        P("member", None, "tile"),
        P("tile"),
        P(),
        P(),
        P(),
        P(),
        P(),
        P(),
        P(),
        P(),
        P(),
    )
    return jax.shard_map(
        body, mesh=mesh, in_specs=placed, out_specs=P("member", None, None, "tile"), check_vma=False
    )
```

```python
import math

import jax
import jax.numpy as jnp
from jax import lax
from jax.experimental import pallas as pl
from jax.experimental.pallas import tpu as pltpu
from jax.sharding import PartitionSpec as P

LAT = 4
WIN = 64
REACH = 1
TRAIN_STEPS = 1000
STRIDE = 20
GROUPS = 32


norm_epsilon = 1e-05
eta_noise = 0.5
beta_first = 0.00085
beta_last = 0.012


def plan_terms(timestep):
    betas_root = jnp.linspace(beta_first**0.5, beta_last**0.5, TRAIN_STEPS, dtype=jnp.float32)
    kept = 1.0 - betas_root * betas_root
    step = jnp.arange(TRAIN_STEPS, dtype=jnp.int32)
    current = jnp.prod(jnp.where(step <= timestep[0], kept, 1.0))
    earlier = jnp.prod(jnp.where(step <= timestep[0] - STRIDE, kept, 1.0))
    sigma_sq = eta_noise * eta_noise * (1.0 - earlier) / (1.0 - current) * (1.0 - current / earlier)
    return (current, earlier, sigma_sq)


def time_embed(timestep, time_weight):
    half_width = time_weight.shape[0] // 2
    freqs_row = jnp.exp(-math.log(10000.0) * jnp.arange(half_width, dtype=jnp.float32) / half_width)
    angles = timestep[0].astype(jnp.float32) * freqs_row
    embedding = jnp.concatenate([jnp.cos(angles), jnp.sin(angles)]).astype(jnp.bfloat16)
    return jax.nn.silu(
        jnp.dot(embedding[None, :], time_weight, preferred_element_type=jnp.float32)[0]
    )


def fold_taps(weight, cin, cin_pad, cout_pad):
    cout = weight.shape[0]
    folded = weight.reshape(cout, 3, 3, cin).transpose(2, 0, 1, 3)
    folded = jnp.pad(folded, ((0, 0), (0, cout_pad - cout), (0, 0), (0, cin_pad - cin)))
    return folded.reshape(3 * cout_pad, 3 * cin_pad)


def conv_cells(activation, folded, cout, row_first, row_last, cell):
    cells = activation.shape[1]
    above = jnp.where(row_first, 0.0, pltpu.roll(activation, 1, 1))
    below = jnp.where(row_last, 0.0, pltpu.roll(activation, cells - 1, 1))
    stacked = jnp.concatenate(
        [above.astype(jnp.bfloat16), activation.astype(jnp.bfloat16), below.astype(jnp.bfloat16)],
        axis=0,
    )
    parts = jnp.dot(folded, stacked, preferred_element_type=jnp.float32)
    left = jnp.where(cell < WIN, 0.0, pltpu.roll(parts[:cout], WIN, 1))
    right = jnp.where(cell >= cells - WIN, 0.0, pltpu.roll(parts[2 * cout :], cells - WIN, 1))
    return parts[cout : 2 * cout] + left + right


def norm_silu(hidden, gain):
    channels, cells = hidden.shape
    size = channels // GROUPS
    lane = (channels, 128)
    row = lax.broadcasted_iota(jnp.int32, lane, 0)

    def group_mean(values):
        total = jnp.broadcast_to(jnp.sum(values, axis=1, keepdims=True), lane)
        step = 1
        while step < size:
            up = pltpu.roll(total, channels - step, 0)
            down = pltpu.roll(total, step, 0)
            total = total + jnp.where((row // step) % 2 == 0, up, down)
            step *= 2
        return total[:, :1] / (size * cells)

    deviate = hidden - group_mean(hidden)
    spread_sq = group_mean(deviate * deviate)
    normed = deviate * (lax.rsqrt(spread_sq + norm_epsilon) * gain)
    return jax.nn.silu(normed).astype(jnp.bfloat16).astype(jnp.float32)


def window_kernel(feature_ref, latent_ref, in_ref, one_ref, two_ref, out_ref, column_ref, eps_ref):
    cells = WIN * WIN
    half = cells // 2
    cell = lax.broadcasted_iota(jnp.int32, (1, cells), 1)
    row = cell % WIN
    marks = (row == 0, row == WIN - 1, cell)
    members = feature_ref.shape[0]
    channels = one_ref.shape[0] // 3
    feature = jnp.concatenate(
        [
            jnp.concatenate([feature_ref[m, h] for m in range(members)], axis=0)
            for h in range(2)
        ],
        axis=1,
    ).astype(jnp.float32)
    latent_win = jnp.concatenate([latent_ref[0], latent_ref[1]], axis=1).astype(jnp.float32)
    gain_one, gain_two, gain_three, time_bias = (column_ref[:, k : k + 1] for k in range(4))
    hidden = conv_cells(latent_win, in_ref[...], channels, *marks) + feature
    act = norm_silu(hidden, gain_one)
    middle = conv_cells(act, one_ref[...], channels, *marks) + time_bias
    act = norm_silu(middle, gain_two)
    block_out = hidden + conv_cells(act, two_ref[...], channels, *marks)
    act = norm_silu(block_out, gain_three)
    eps = conv_cells(act, out_ref[...], out_ref.shape[0] // 3, *marks)
    eps_ref[0] = eps[:LAT, :half]
    eps_ref[1] = eps[:LAT, half:]


def denoise_windows(feature, latent_win, folded, columns):
    members, halves, share, half = feature.shape
    padded = latent_win.shape[1]
    whole = [pl.BlockSpec(f.shape, lambda s: (0, 0)) for f in (*folded, columns)]
    slots = halves // 2
    return pl.pallas_call(
        window_kernel,
        grid=(slots,),
        in_specs=[
            pl.BlockSpec((members, 2, share, half), lambda s: (0, s, 0, 0)),
            pl.BlockSpec((2, padded, half), lambda s: (s, 0, 0)),
            *whole,
        ],
        out_specs=pl.BlockSpec((2, LAT, half), lambda s: (s, 0, 0)),
        out_shape=jax.ShapeDtypeStruct((halves, LAT, half), jnp.float32),
        compiler_params=pltpu.CompilerParams(vmem_limit_bytes=50 * 2**20),
        cost_estimate=pl.CostEstimate(
            flops=slots * 2 * sum(f.size for f in folded) * 2 * half,
            bytes_accessed=2 * feature.size,
            transcendentals=0,
        ),
    )(feature, latent_win, *folded, columns)


def pick_kernel(wanted_ref, block_ref, *picked_refs):
    for which, picked_ref in enumerate(picked_refs):
        for k in range(picked_ref.shape[0]):
            picked_ref[k] = block_ref[wanted_ref[which, k]]


def pick_blocks(wanted, blocks):
    shape = jax.ShapeDtypeStruct((wanted.shape[1], *blocks.shape[1:]), blocks.dtype)
    return pl.pallas_call(
        pick_kernel,
        in_specs=[
            pl.BlockSpec(memory_space=pltpu.SMEM),
            pl.BlockSpec(memory_space=pltpu.VMEM),
        ],
        out_specs=[pl.BlockSpec(memory_space=pltpu.VMEM)] * wanted.shape[0],
        out_shape=[shape] * wanted.shape[0],
        compiler_params=pltpu.CompilerParams(vmem_limit_bytes=24 * 2**20),
    )(wanted, blocks)


def shift_tiles(value, by):
    count = lax.axis_size("tile")
    return lax.ppermute(
        value, "tile", [(i, i + by) for i in range(count) if 0 <= i + by < count]
    )


def by_blocks(array, half_win):
    channels, rows, width = array.shape
    split = array.reshape(channels, rows, width // half_win, half_win)
    return split.transpose(2, 0, 3, 1).reshape(width // half_win, channels, half_win * rows)


def denoise_update(state_now, eps_mean, noise_draw, current, earlier, sigma_sq):
    clean_est = (state_now - jnp.sqrt(1.0 - current) * eps_mean) / jnp.sqrt(current)
    return (
        jnp.sqrt(earlier) * clean_est
        + jnp.sqrt(1.0 - earlier - sigma_sq) * eps_mean
        + jnp.sqrt(sigma_sq) * noise_draw
    )


def body(
    latent,
    noise,
    features,
    slot_window,
    timestep,
    time_weight,
    in_weight,
    conv1_weight,
    conv2_weight,
    out_weight,
    norm1_gain,
    norm2_gain,
    norm3_gain,
):
    tile_width = latent.shape[-1]
    half_win = WIN // 2
    per_tile = tile_width // half_win
    tile_index = lax.axis_index("tile")
    slots_low = shift_tiles(slot_window + 1, 1) - 1
    slots_high = shift_tiles(slot_window + 1, -1) - 1

    def places(slots):
        start = slots - tile_index * per_tile
        return jnp.stack([start, start + 1], axis=1).reshape(-1)

    feature_blocks = by_blocks(features, half_win)
    latent_blocks = by_blocks(latent[0].astype(jnp.bfloat16), half_win)
    own = places(slot_window)
    low = places(slots_low)
    high = places(slots_high)

    wanted = jnp.clip(jnp.stack([own, low, high]), 0, per_tile - 1)
    mine = own[:, None, None]

    def listed_blocks(picked):
        from_high = shift_tiles(picked[1], -1)
        from_low = shift_tiles(picked[2], 1)
        return jnp.where(mine < 0, from_low, jnp.where(mine >= per_tile, from_high, picked[0]))

    feature_win = lax.all_gather(
        listed_blocks(pick_blocks(wanted, feature_blocks)), "member", axis=0
    )
    latent_win = listed_blocks(pick_blocks(wanted, latent_blocks))
    pad = 16 - LAT
    latent_win = jnp.pad(latent_win, ((0, 0), (0, pad), (0, 0)))
    current, earlier, sigma_sq = plan_terms(timestep)
    time_bias = time_embed(timestep, time_weight)
    channels = in_weight.shape[0]
    folded = (
        fold_taps(in_weight, LAT, LAT + pad, channels),
        fold_taps(conv1_weight, channels, channels, channels),
        fold_taps(conv2_weight, channels, channels, channels),
        fold_taps(out_weight, channels, channels, 8),
    )
    columns = jnp.stack([norm1_gain, norm2_gain, norm3_gain, time_bias] * 2, axis=1)
    eps = denoise_windows(feature_win, latent_win, folded, columns)
    halves = eps.shape[0]
    eps_link = eps.astype(jnp.bfloat16)
    eps_all = jnp.concatenate(
        [
            eps,
            shift_tiles(eps_link, 1).astype(jnp.float32),
            shift_tiles(eps_link, -1).astype(jnp.float32),
        ]
    )
    place = jnp.concatenate([own, low, high])
    listed = jnp.repeat(jnp.concatenate([slot_window, slots_low, slots_high]) >= 0, 2)
    block_ids = jnp.arange(per_tile, dtype=jnp.int32)
    hit = ((place[None, :] == block_ids[:, None]) & listed[None, :]).astype(jnp.float32)
    cover = jnp.sum(hit, axis=1)
    total = jnp.dot(
        hit,
        eps_all.reshape(3 * halves, -1),
        precision=lax.Precision.HIGHEST,
        preferred_element_type=jnp.float32,
    )
    eps_mean = total / jnp.maximum(cover, 1.0)[:, None]
    eps_mean = (
        eps_mean.reshape(per_tile, LAT, half_win, WIN)
        .transpose(1, 3, 0, 2)
        .reshape(LAT, WIN, tile_width)
    )
    return denoise_update(latent[0], eps_mean, noise[0], current, earlier, sigma_sq)[None]


def solution(mesh):
    placed = (
        P("member", None, None, "tile"),
        P("member", None, None, "tile"),
        P("member", None, "tile"),
        P("tile"),
        P(),
        P(),
        P(),
        P(),
        P(),
        P(),
        P(),
        P(),
        P(),
    )
    return jax.shard_map(
        body, mesh=mesh, in_specs=placed, out_specs=P("member", None, None, "tile"), check_vma=False
    )
```

```python
import functools
import math

import jax
import jax.numpy as jnp
from jax import lax
from jax.experimental import pallas as pl
from jax.experimental.pallas import tpu as pltpu
from jax.sharding import PartitionSpec as P

LAT = 4
WIN = 64
REACH = 1
TRAIN_STEPS = 1000
STRIDE = 20
GROUPS = 32
PIECES = 2


norm_epsilon = 1e-05
eta_noise = 0.5
beta_first = 0.00085
beta_last = 0.012


def plan_terms(timestep):
    betas_root = jnp.linspace(beta_first**0.5, beta_last**0.5, TRAIN_STEPS, dtype=jnp.float32)
    kept = 1.0 - betas_root * betas_root
    step = jnp.arange(TRAIN_STEPS, dtype=jnp.int32)
    current = jnp.prod(jnp.where(step <= timestep[0], kept, 1.0))
    earlier = jnp.prod(jnp.where(step <= timestep[0] - STRIDE, kept, 1.0))
    sigma_sq = eta_noise * eta_noise * (1.0 - earlier) / (1.0 - current) * (1.0 - current / earlier)
    return (current, earlier, sigma_sq)


def time_embed(timestep, time_weight):
    half_width = time_weight.shape[0] // 2
    freqs_row = jnp.exp(-math.log(10000.0) * jnp.arange(half_width, dtype=jnp.float32) / half_width)
    angles = timestep[0].astype(jnp.float32) * freqs_row
    embedding = jnp.concatenate([jnp.cos(angles), jnp.sin(angles)]).astype(jnp.bfloat16)
    return jax.nn.silu(
        jnp.dot(embedding[None, :], time_weight, preferred_element_type=jnp.float32)[0]
    )


def fold_taps(weight, cin, cin_pad, cout_pad):
    cout = weight.shape[0]
    folded = weight.reshape(cout, 3, 3, cin).transpose(2, 0, 1, 3)
    folded = jnp.pad(folded, ((0, 0), (0, cout_pad - cout), (0, 0), (0, cin_pad - cin)))
    return folded.reshape(3 * cout_pad, 3 * cin_pad)


def conv_cells(activation, folded, cout, row_first, row_last, cell):
    cells = activation.shape[1]
    above = jnp.where(row_first, 0.0, pltpu.roll(activation, 1, 1))
    below = jnp.where(row_last, 0.0, pltpu.roll(activation, cells - 1, 1))
    stacked = jnp.concatenate(
        [above.astype(jnp.bfloat16), activation.astype(jnp.bfloat16), below.astype(jnp.bfloat16)],
        axis=0,
    )
    parts = jnp.dot(folded, stacked, preferred_element_type=jnp.float32)
    left = jnp.where(cell < WIN, 0.0, pltpu.roll(parts[:cout], WIN, 1))
    right = jnp.where(cell >= cells - WIN, 0.0, pltpu.roll(parts[2 * cout :], cells - WIN, 1))
    return parts[cout : 2 * cout] + left + right


def norm_silu(hidden, gain):
    channels, cells = hidden.shape
    size = channels // GROUPS
    lane = (channels, 128)
    row = lax.broadcasted_iota(jnp.int32, lane, 0)

    def group_mean(values):
        total = jnp.broadcast_to(jnp.sum(values, axis=1, keepdims=True), lane)
        step = 1
        while step < size:
            up = pltpu.roll(total, channels - step, 0)
            down = pltpu.roll(total, step, 0)
            total = total + jnp.where((row // step) % 2 == 0, up, down)
            step *= 2
        return total[:, :1] / (size * cells)

    deviate = hidden - group_mean(hidden)
    spread_sq = group_mean(deviate * deviate)
    normed = deviate * (lax.rsqrt(spread_sq + norm_epsilon) * gain)
    return jax.nn.silu(normed).astype(jnp.bfloat16).astype(jnp.float32)


def window_kernel(feature_ref, latent_ref, in_ref, one_ref, two_ref, out_ref, column_ref, eps_ref):
    cells = WIN * WIN
    half = cells // 2
    cell = lax.broadcasted_iota(jnp.int32, (1, cells), 1)
    row = cell % WIN
    marks = (row == 0, row == WIN - 1, cell)
    members = feature_ref.shape[0]
    channels = one_ref.shape[0] // 3
    feature = jnp.concatenate(
        [
            jnp.concatenate([feature_ref[m, h] for m in range(members)], axis=0)
            for h in range(2)
        ],
        axis=1,
    ).astype(jnp.float32)
    latent_win = jnp.concatenate([latent_ref[0], latent_ref[1]], axis=1).astype(jnp.float32)
    gain_one, gain_two, gain_three, time_bias = (column_ref[:, k : k + 1] for k in range(4))
    hidden = conv_cells(latent_win, in_ref[...], channels, *marks) + feature
    act = norm_silu(hidden, gain_one)
    middle = conv_cells(act, one_ref[...], channels, *marks) + time_bias
    act = norm_silu(middle, gain_two)
    block_out = hidden + conv_cells(act, two_ref[...], channels, *marks)
    act = norm_silu(block_out, gain_three)
    eps = conv_cells(act, out_ref[...], out_ref.shape[0] // 3, *marks)
    eps_ref[0] = eps[:LAT, :half]
    eps_ref[1] = eps[:LAT, half:]


def denoise_windows(feature, latent_win, folded, columns):
    members, halves, share, half = feature.shape
    padded = latent_win.shape[1]
    whole = [pl.BlockSpec(f.shape, lambda s: (0, 0)) for f in (*folded, columns)]
    slots = halves // 2
    return pl.pallas_call(
        window_kernel,
        grid=(slots,),
        in_specs=[
            pl.BlockSpec((members, 2, share, half), lambda s: (0, s, 0, 0)),
            pl.BlockSpec((2, padded, half), lambda s: (s, 0, 0)),
            *whole,
        ],
        out_specs=pl.BlockSpec((2, LAT, half), lambda s: (s, 0, 0)),
        out_shape=jax.ShapeDtypeStruct((halves, LAT, half), jnp.float32),
        compiler_params=pltpu.CompilerParams(vmem_limit_bytes=50 * 2**20),
        cost_estimate=pl.CostEstimate(
            flops=slots * 2 * sum(f.size for f in folded) * 2 * half,
            bytes_accessed=2 * feature.size,
            transcendentals=0,
        ),
    )(feature, latent_win, *folded, columns)


def pick_kernel(sizes, wanted_ref, *refs):
    source_refs, picked_refs = refs[: len(sizes)], refs[len(sizes) :]
    kinds = wanted_ref.shape[0]
    for index, picked_ref in enumerate(picked_refs):
        piece, kind = divmod(index, kinds)
        count = picked_ref.shape[0]
        for k in range(count):
            block = wanted_ref[kind, piece * count + k]
            low = 0
            for source_ref, size in zip(source_refs, sizes):
                at = pl.multiple_of(block * size, size)
                picked_ref[k, :, low : low + size] = source_ref[:, pl.ds(at, size)]
                low += size


def pick_blocks(wanted, sources, pieces, sizes):
    kinds, count = wanted.shape
    rows = sources[0].shape[0]
    shape = jax.ShapeDtypeStruct((count // pieces, rows, sum(sizes)), sources[0].dtype)
    outs = kinds * pieces
    picked = pl.pallas_call(
        functools.partial(pick_kernel, sizes),
        in_specs=[pl.BlockSpec(memory_space=pltpu.SMEM)]
        + [pl.BlockSpec(memory_space=pltpu.VMEM)] * len(sources),
        out_specs=[pl.BlockSpec(memory_space=pltpu.VMEM)] * outs,
        out_shape=[shape] * outs,
        compiler_params=pltpu.CompilerParams(vmem_limit_bytes=24 * 2**20),
    )(wanted, *sources)
    return [picked[p * kinds : (p + 1) * kinds] for p in range(pieces)]


def shift_tiles(value, by):
    count = lax.axis_size("tile")
    return lax.ppermute(
        value, "tile", [(i, i + by) for i in range(count) if 0 <= i + by < count]
    )


def by_columns(array):
    return array.transpose(0, 2, 1).reshape(array.shape[0], -1)


def denoise_update(state_now, eps_mean, noise_draw, current, earlier, sigma_sq):
    clean_est = (state_now - jnp.sqrt(1.0 - current) * eps_mean) / jnp.sqrt(current)
    return (
        jnp.sqrt(earlier) * clean_est
        + jnp.sqrt(1.0 - earlier - sigma_sq) * eps_mean
        + jnp.sqrt(sigma_sq) * noise_draw
    )


def body(
    latent,
    noise,
    features,
    slot_window,
    timestep,
    time_weight,
    in_weight,
    conv1_weight,
    conv2_weight,
    out_weight,
    norm1_gain,
    norm2_gain,
    norm3_gain,
):
    tile_width = latent.shape[-1]
    half_win = WIN // 2
    per_tile = tile_width // half_win
    tile_index = lax.axis_index("tile")
    slots_low = shift_tiles(slot_window + 1, 1) - 1
    slots_high = shift_tiles(slot_window + 1, -1) - 1

    def places(slots):
        start = slots - tile_index * per_tile
        return jnp.stack([start, start + 1], axis=1).reshape(-1)

    pieces = math.gcd(slot_window.shape[0], PIECES)
    feature_cells = by_columns(features)
    latent_cells = by_columns(latent[0].astype(jnp.bfloat16))
    own = places(slot_window)
    low = places(slots_low)
    high = places(slots_high)

    wanted = jnp.clip(jnp.stack([own, low, high]), 0, per_tile - 1)
    mine = jnp.split(own[:, None, None], pieces)
    half = half_win * WIN

    def listed_blocks(piece, picked):
        from_high = shift_tiles(picked[1], -1)
        from_low = shift_tiles(picked[2], 1)
        at = mine[piece]
        return jnp.where(at < 0, from_low, jnp.where(at >= per_tile, from_high, picked[0]))

    share = features.shape[0]
    folds = share // LAT
    thin = half // folds
    latent_cells = (
        latent_cells.reshape(LAT, per_tile, folds, thin)
        .transpose(2, 0, 1, 3)
        .reshape(share, per_tile * thin)
    )
    pad = 16 - LAT
    feature_wins, latent_wins = [], []
    picks = pick_blocks(wanted, (feature_cells, latent_cells), pieces, (half, thin))
    for piece, picked in enumerate(picks):
        both = listed_blocks(piece, picked)
        feature_wins.append(lax.all_gather(both[:, :, :half], "member", axis=0))
        latent_win = both[:, :, half:].reshape(-1, folds, LAT, thin).transpose(0, 2, 1, 3)
        latent_wins.append(
            jnp.pad(latent_win.reshape(-1, LAT, half), ((0, 0), (0, pad), (0, 0)))
        )
    current, earlier, sigma_sq = plan_terms(timestep)
    time_bias = time_embed(timestep, time_weight)
    channels = in_weight.shape[0]
    folded = (
        fold_taps(in_weight, LAT, LAT + pad, channels),
        fold_taps(conv1_weight, channels, channels, channels),
        fold_taps(conv2_weight, channels, channels, channels),
        fold_taps(out_weight, channels, channels, 8),
    )
    columns = jnp.stack([norm1_gain, norm2_gain, norm3_gain, time_bias] * 2, axis=1)
    eps = jnp.concatenate(
        [
            denoise_windows(feature_win, latent_win, folded, columns)
            for feature_win, latent_win in zip(feature_wins, latent_wins)
        ]
    )
    link = eps.astype(jnp.bfloat16)
    eps_all = jnp.concatenate(
        [
            eps,
            shift_tiles(link, 1).astype(jnp.float32),
            shift_tiles(link, -1).astype(jnp.float32),
        ]
    )
    halves = own.shape[0]
    place = jnp.concatenate([own, low, high])
    listed = jnp.repeat(jnp.concatenate([slot_window, slots_low, slots_high]) >= 0, 2)
    block_ids = jnp.arange(per_tile, dtype=jnp.int32)
    hit = ((place[None, :] == block_ids[:, None]) & listed[None, :]).astype(jnp.float32)
    cover = jnp.sum(hit, axis=1)
    total = jnp.dot(
        hit,
        eps_all.reshape(3 * halves, -1),
        precision=lax.Precision.HIGHEST,
        preferred_element_type=jnp.float32,
    )
    eps_mean = total / jnp.maximum(cover, 1.0)[:, None]
    eps_mean = (
        eps_mean.reshape(per_tile, LAT, half_win, WIN)
        .transpose(1, 3, 0, 2)
        .reshape(LAT, WIN, tile_width)
    )
    eps_mean = lax.optimization_barrier(eps_mean)
    return denoise_update(latent[0], eps_mean, noise[0], current, earlier, sigma_sq)[None]


def solution(mesh):
    placed = (
        P("member", None, None, "tile"),
        P("member", None, None, "tile"),
        P("member", None, "tile"),
        P("tile"),
        P(),
        P(),
        P(),
        P(),
        P(),
        P(),
        P(),
        P(),
        P(),
    )
    return jax.shard_map(
        body, mesh=mesh, in_specs=placed, out_specs=P("member", None, None, "tile"), check_vma=False
    )
```

```python
import functools
import math

import jax
import jax.numpy as jnp
from jax import lax
from jax.experimental import pallas as pl
from jax.experimental.pallas import tpu as pltpu
from jax.sharding import PartitionSpec as P

LAT = 4
WIN = 64
REACH = 1
TRAIN_STEPS = 1000
STRIDE = 20
GROUPS = 32
PIECES = 2


norm_epsilon = 1e-05
eta_noise = 0.5
beta_first = 0.00085
beta_last = 0.012


def plan_terms(timestep):
    betas_root = jnp.linspace(beta_first**0.5, beta_last**0.5, TRAIN_STEPS, dtype=jnp.float32)
    kept = 1.0 - betas_root * betas_root
    step = jnp.arange(TRAIN_STEPS, dtype=jnp.int32)
    current = jnp.prod(jnp.where(step <= timestep[0], kept, 1.0))
    earlier = jnp.prod(jnp.where(step <= timestep[0] - STRIDE, kept, 1.0))
    sigma_sq = eta_noise * eta_noise * (1.0 - earlier) / (1.0 - current) * (1.0 - current / earlier)
    return (current, earlier, sigma_sq)


def time_embed(timestep, time_weight):
    half_width = time_weight.shape[0] // 2
    freqs_row = jnp.exp(-math.log(10000.0) * jnp.arange(half_width, dtype=jnp.float32) / half_width)
    angles = timestep[0].astype(jnp.float32) * freqs_row
    embedding = jnp.concatenate([jnp.cos(angles), jnp.sin(angles)]).astype(jnp.bfloat16)
    return jax.nn.silu(
        jnp.dot(embedding[None, :], time_weight, preferred_element_type=jnp.float32)[0]
    )


def fold_taps(weight, cin, cin_pad, cout_pad):
    cout = weight.shape[0]
    folded = weight.reshape(cout, 3, 3, cin).transpose(2, 0, 1, 3)
    folded = jnp.pad(folded, ((0, 0), (0, cout_pad - cout), (0, 0), (0, cin_pad - cin)))
    return folded.reshape(3 * cout_pad, 3 * cin_pad)


def conv_cells(activation, folded, cout, row_first, row_last, cell):
    cells = activation.shape[1]
    above = jnp.where(row_first, 0.0, pltpu.roll(activation, 1, 1))
    below = jnp.where(row_last, 0.0, pltpu.roll(activation, cells - 1, 1))
    stacked = jnp.concatenate(
        [above.astype(jnp.bfloat16), activation.astype(jnp.bfloat16), below.astype(jnp.bfloat16)],
        axis=0,
    )
    parts = jnp.dot(folded, stacked, preferred_element_type=jnp.float32)
    left = jnp.where(cell < WIN, 0.0, pltpu.roll(parts[:cout], WIN, 1))
    right = jnp.where(cell >= cells - WIN, 0.0, pltpu.roll(parts[2 * cout :], cells - WIN, 1))
    return parts[cout : 2 * cout] + left + right


def norm_silu(hidden, gain):
    channels, cells = hidden.shape
    size = channels // GROUPS
    lane = (channels, 128)
    row = lax.broadcasted_iota(jnp.int32, lane, 0)

    def group_mean(values):
        total = jnp.broadcast_to(jnp.sum(values, axis=1, keepdims=True), lane)
        step = 1
        while step < size:
            up = pltpu.roll(total, channels - step, 0)
            down = pltpu.roll(total, step, 0)
            total = total + jnp.where((row // step) % 2 == 0, up, down)
            step *= 2
        return total[:, :1] / (size * cells)

    deviate = hidden - group_mean(hidden)
    spread_sq = group_mean(deviate * deviate)
    normed = deviate * (lax.rsqrt(spread_sq + norm_epsilon) * gain)
    return jax.nn.silu(normed).astype(jnp.bfloat16).astype(jnp.float32)


def window_kernel(feature_ref, latent_ref, in_ref, one_ref, two_ref, out_ref, column_ref, eps_ref):
    cells = WIN * WIN
    half = cells // 2
    cell = lax.broadcasted_iota(jnp.int32, (1, cells), 1)
    row = cell % WIN
    marks = (row == 0, row == WIN - 1, cell)
    members = feature_ref.shape[0]
    channels = one_ref.shape[0] // 3
    feature = jnp.concatenate(
        [
            jnp.concatenate([feature_ref[m, h] for m in range(members)], axis=0)
            for h in range(2)
        ],
        axis=1,
    ).astype(jnp.float32)
    packed = [latent_ref[h].astype(jnp.float32) for h in range(2)]
    folds = packed[0].shape[0] // LAT
    latent_win = jnp.concatenate(
        [p[LAT * q : LAT * (q + 1)] for p in packed for q in range(folds)], axis=1
    )
    spare = in_ref.shape[1] // 3 - LAT
    latent_win = jnp.concatenate([latent_win, jnp.zeros((spare, cells), jnp.float32)], axis=0)
    gain_one, gain_two, gain_three, time_bias = (column_ref[:, k : k + 1] for k in range(4))
    hidden = conv_cells(latent_win, in_ref[...], channels, *marks) + feature
    act = norm_silu(hidden, gain_one)
    middle = conv_cells(act, one_ref[...], channels, *marks) + time_bias
    act = norm_silu(middle, gain_two)
    block_out = hidden + conv_cells(act, two_ref[...], channels, *marks)
    act = norm_silu(block_out, gain_three)
    eps = conv_cells(act, out_ref[...], out_ref.shape[0] // 3, *marks)
    eps_ref[0] = eps[:LAT, :half]
    eps_ref[1] = eps[:LAT, half:]


def denoise_windows(feature, latent_win, folded, columns):
    members, halves, share, half = feature.shape
    whole = [pl.BlockSpec(f.shape, lambda s: (0, 0)) for f in (*folded, columns)]
    slots = halves // 2
    return pl.pallas_call(
        window_kernel,
        grid=(slots,),
        in_specs=[
            pl.BlockSpec((members, 2, share, half), lambda s: (0, s, 0, 0)),
            pl.BlockSpec((2, *latent_win.shape[1:]), lambda s: (s, 0, 0)),
            *whole,
        ],
        out_specs=pl.BlockSpec((2, LAT, half), lambda s: (s, 0, 0)),
        out_shape=jax.ShapeDtypeStruct((halves, LAT, half), jnp.float32),
        compiler_params=pltpu.CompilerParams(vmem_limit_bytes=50 * 2**20),
        cost_estimate=pl.CostEstimate(
            flops=slots * 2 * sum(f.size for f in folded) * 2 * half,
            bytes_accessed=2 * feature.size,
            transcendentals=0,
        ),
    )(feature, latent_win, *folded, columns)


def pick_kernel(sizes, wanted_ref, *refs):
    source_refs, picked_refs = refs[: len(sizes)], refs[len(sizes) :]
    kinds = wanted_ref.shape[0]
    for index, picked_ref in enumerate(picked_refs):
        piece, kind = divmod(index, kinds)
        count = picked_ref.shape[0]
        for k in range(count):
            block = wanted_ref[kind, piece * count + k]
            low = 0
            for source_ref, size in zip(source_refs, sizes):
                at = pl.multiple_of(block * size, size)
                picked_ref[k, :, low : low + size] = source_ref[:, pl.ds(at, size)]
                low += size


def pick_blocks(wanted, sources, pieces, sizes):
    kinds, count = wanted.shape
    rows = sources[0].shape[0]
    shape = jax.ShapeDtypeStruct((count // pieces, rows, sum(sizes)), sources[0].dtype)
    outs = kinds * pieces
    picked = pl.pallas_call(
        functools.partial(pick_kernel, sizes),
        in_specs=[pl.BlockSpec(memory_space=pltpu.SMEM)]
        + [pl.BlockSpec(memory_space=pltpu.VMEM)] * len(sources),
        out_specs=[pl.BlockSpec(memory_space=pltpu.VMEM)] * outs,
        out_shape=[shape] * outs,
        compiler_params=pltpu.CompilerParams(vmem_limit_bytes=24 * 2**20),
    )(wanted, *sources)
    return [picked[p * kinds : (p + 1) * kinds] for p in range(pieces)]


def shift_tiles(value, by):
    count = lax.axis_size("tile")
    return lax.ppermute(
        value, "tile", [(i, i + by) for i in range(count) if 0 <= i + by < count]
    )


def by_columns(array):
    return array.transpose(0, 2, 1).reshape(array.shape[0], -1)


def denoise_update(state_now, eps_mean, noise_draw, current, earlier, sigma_sq):
    clean_est = (state_now - jnp.sqrt(1.0 - current) * eps_mean) / jnp.sqrt(current)
    return (
        jnp.sqrt(earlier) * clean_est
        + jnp.sqrt(1.0 - earlier - sigma_sq) * eps_mean
        + jnp.sqrt(sigma_sq) * noise_draw
    )


def body(
    latent,
    noise,
    features,
    slot_window,
    timestep,
    time_weight,
    in_weight,
    conv1_weight,
    conv2_weight,
    out_weight,
    norm1_gain,
    norm2_gain,
    norm3_gain,
):
    tile_width = latent.shape[-1]
    half_win = WIN // 2
    per_tile = tile_width // half_win
    tile_index = lax.axis_index("tile")
    slots_low = shift_tiles(slot_window + 1, 1) - 1
    slots_high = shift_tiles(slot_window + 1, -1) - 1

    def places(slots):
        start = slots - tile_index * per_tile
        return jnp.stack([start, start + 1], axis=1).reshape(-1)

    pieces = math.gcd(slot_window.shape[0], PIECES)
    feature_cells = by_columns(features)
    latent_cells = by_columns(latent[0].astype(jnp.bfloat16))
    own = places(slot_window)
    low = places(slots_low)
    high = places(slots_high)

    wanted = jnp.clip(jnp.stack([own, low, high]), 0, per_tile - 1)
    mine = jnp.split(own[:, None, None], pieces)
    half = half_win * WIN

    def listed_blocks(piece, picked):
        from_high = shift_tiles(picked[1], -1)
        from_low = shift_tiles(picked[2], 1)
        at = mine[piece]
        return jnp.where(at < 0, from_low, jnp.where(at >= per_tile, from_high, picked[0]))

    share = features.shape[0]
    folds = share // LAT
    thin = half // folds
    latent_cells = (
        latent_cells.reshape(LAT, per_tile, folds, thin)
        .transpose(2, 0, 1, 3)
        .reshape(share, per_tile * thin)
    )
    pad = 16 - LAT
    feature_wins, latent_wins = [], []
    picks = pick_blocks(wanted, (feature_cells, latent_cells), pieces, (half, thin))
    for piece, picked in enumerate(picks):
        both = listed_blocks(piece, picked)
        feature_wins.append(lax.all_gather(both[:, :, :half], "member", axis=0))
        latent_wins.append(both[:, :, half:])
    current, earlier, sigma_sq = plan_terms(timestep)
    time_bias = time_embed(timestep, time_weight)
    channels = in_weight.shape[0]
    folded = (
        fold_taps(in_weight, LAT, LAT + pad, channels),
        fold_taps(conv1_weight, channels, channels, channels),
        fold_taps(conv2_weight, channels, channels, channels),
        fold_taps(out_weight, channels, channels, 8),
    )
    columns = jnp.stack([norm1_gain, norm2_gain, norm3_gain, time_bias] * 2, axis=1)
    eps = jnp.concatenate(
        [
            denoise_windows(feature_win, latent_win, folded, columns)
            for feature_win, latent_win in zip(feature_wins, latent_wins)
        ]
    )
    link = eps.astype(jnp.bfloat16)
    eps_all = jnp.concatenate(
        [
            eps,
            shift_tiles(link, 1).astype(jnp.float32),
            shift_tiles(link, -1).astype(jnp.float32),
        ]
    )
    halves = own.shape[0]
    place = jnp.concatenate([own, low, high])
    listed = jnp.repeat(jnp.concatenate([slot_window, slots_low, slots_high]) >= 0, 2)
    block_ids = jnp.arange(per_tile, dtype=jnp.int32)
    hit = ((place[None, :] == block_ids[:, None]) & listed[None, :]).astype(jnp.float32)
    cover = jnp.sum(hit, axis=1)
    total = jnp.dot(
        hit,
        eps_all.reshape(3 * halves, -1),
        precision=lax.Precision.HIGHEST,
        preferred_element_type=jnp.float32,
    )
    eps_mean = total / jnp.maximum(cover, 1.0)[:, None]
    eps_mean = (
        eps_mean.reshape(per_tile, LAT, half_win, WIN)
        .transpose(1, 3, 0, 2)
        .reshape(LAT, WIN, tile_width)
    )
    eps_mean = lax.optimization_barrier(eps_mean)
    return denoise_update(latent[0], eps_mean, noise[0], current, earlier, sigma_sq)[None]


def solution(mesh):
    placed = (
        P("member", None, None, "tile"),
        P("member", None, None, "tile"),
        P("member", None, "tile"),
        P("tile"),
        P(),
        P(),
        P(),
        P(),
        P(),
        P(),
        P(),
        P(),
        P(),
    )
    return jax.shard_map(
        body, mesh=mesh, in_specs=placed, out_specs=P("member", None, None, "tile"), check_vma=False
    )
```
